512 devices in a mesh: dp: 128 (over x, z_lo, y), mp: 2 (over core), gen: 2 (over z_hi).
Axes of the slice: x: 4, y: 4, z: 16 (z_hi: 2, z_lo: 8; z = z_hi * 8 + z_lo), core: 2. Of those that a mesh axis runs over, the one named last changes fastest.
Arguments:
- fresh_tokens: bfloat16 [32768, 1536], P(('dp', 'gen')), may hold values from -6 to 6
- saved_tokens: bfloat16 [32768, 1536], P('dp'), may hold values from -6 to 6
- cotangents: bfloat16 [2, 32768, 1536], P(None, 'dp', ('mp', 'gen')), may hold values from -20 to 20
- feedback: bfloat16 [2, 128, 1536, 1536], P(None, 'dp', None, ('mp', 'gen')), may hold values from -6 to 6
- start_factors: bfloat16 [2, 1536, 32], P(None, ('mp', 'gen')), may hold values from -6 to 6
Outputs:
- row_basis: float32 [2, 1536, 32], replicated
- col_factors: float32 [2, 1536, 32], P(None, ('mp', 'gen'))
The draws below stay inside these ranges and needn't reach their ends.
All inputs are finite; a program needn't handle non-finite values.
Results may differ from the reference program's by a relative error of at most 0.0033.
Values may be sent and summed in bfloat16 or wider, within the bound.
A program may use at most 64 MiB of HBM per device.

```python
import math
import jax
import jax.numpy as jnp
from jax import lax

D_IN = 1536
D_OUT = 1536
RANK = 32
LAYERS = 2
TOK_DEV = 256
TOKENS = 32768
N_DP = 128


def draw_cotangents(key, part):
    key = jax.random.fold_in(key, 7)
    keys = jax.random.split(key, 3)
    shape = (LAYERS, TOKENS, D_OUT)
    rising = 10.0 ** (jnp.arange(TOKENS, dtype=jnp.float32) / TOKENS)
    row_scale = rising[None, :, None] * jax.random.uniform(keys[1], (LAYERS, TOKENS, 1), jnp.float32, 0.5, 1.5)
    col_scale = jnp.exp(jax.random.uniform(keys[2], (LAYERS, 1, D_OUT), jnp.float32) * jnp.log(10.0))
    base = jnp.clip(jax.random.normal(keys[0], shape, jnp.float32), -5.0, 5.0)
    return (0.02 * base * row_scale * col_scale).astype(jnp.bfloat16)


def shard_levels(own_key, extent, cuts, least, largest):
    loudness, own = 1.0, jax.random.fold_in(own_key, 6)
    for axis_at, blocks in cuts:
        draws = jnp.exp(jax.random.uniform(jax.random.fold_in(own, axis_at), (blocks,), jnp.float32, least / len(cuts), largest / len(cuts)))
        loudness = loudness * jnp.repeat(draws, extent[axis_at] // blocks).reshape([-1 if axis == axis_at else 1 for axis in range(len(extent))])
    return loudness


def noise(key, shape, deviation, most, pieces=(), held_as=jnp.bfloat16):
    drawn = jax.random.normal(key, shape, jnp.float32) * deviation
    if len(pieces) > 0:
        drawn = shard_levels(key, shape, pieces, -0.22, 0.18) * drawn
    return jnp.clip(drawn, min=-most, max=most).astype(held_as)


def setup_inputs(seed: int = 0) -> dict:
    seeds = jax.random.split(jax.random.key(seed), 6)
    return {
        "fresh_tokens": noise(seeds[0], (TOKENS, D_IN), 1.0, 6.0, ((0, 256),)),
        "saved_tokens": noise(seeds[1], (TOKENS, D_IN), 1.0, 6.0, ((0, 128),)),
        "cotangents": draw_cotangents(jax.random.fold_in(seeds[5], 71), 0),
        "feedback": noise(seeds[3], (LAYERS, N_DP, D_IN, D_OUT), 1.0, 6.0, ((1, 128), (3, 4))),
        "start_factors": noise(seeds[4], (LAYERS, D_OUT, RANK), 1.0, 6.0, ((1, 4),)),
    }


def compensated(tokens, grads, carried):
    grad_sum = jnp.dot(tokens.T.astype(jnp.float32), grads.astype(jnp.float32), preferred_element_type=jnp.float32)
    return (grad_sum + carried.astype(jnp.float32)).astype(jnp.bfloat16)

def reference(fresh_tokens, saved_tokens, cotangents, feedback, start_factors):
    highest = lax.Precision.HIGHEST
    bases = []
    factors = []
    replicas = jnp.arange(N_DP).astype(jnp.int32)
    for which in range(LAYERS):
        inputs = fresh_tokens if which == 0 else saved_tokens
        grads_all = cotangents[which]

        def replica_matrix(replica):
            first_row = (replica * TOK_DEV).astype(jnp.int32)
            tokens = lax.dynamic_slice_in_dim(inputs, first_row, TOK_DEV, 0)
            grads = lax.dynamic_slice_in_dim(grads_all, first_row, TOK_DEV, 0)
            return compensated(tokens, grads, feedback[which, replica])

        def power_step(total, replica):
            matrix = replica_matrix(replica)
            return (total + jnp.dot(matrix.astype(jnp.float32), start_factors[which].astype(jnp.float32), preferred_element_type=jnp.float32), None)
        power, _ = lax.scan(power_step, jnp.zeros((D_IN, RANK), jnp.float32), replicas)
        gram_matrix = jnp.dot(power.T, power, precision=highest)
        lower_factor = jnp.linalg.cholesky(gram_matrix)
        basis = jax.scipy.linalg.solve_triangular(lower_factor, power.T, lower=True).T
        basis_half = basis.astype(jnp.bfloat16)

        def coeff_step(total, replica):
            matrix = replica_matrix(replica)
            return (total + jnp.dot(matrix.T.astype(jnp.float32), basis_half.astype(jnp.float32), preferred_element_type=jnp.float32), None)
        coeffs, _ = lax.scan(coeff_step, jnp.zeros((D_OUT, RANK), jnp.float32), replicas)
        bases.append(math.sqrt(D_IN) * basis)
        factors.append(coeffs / N_DP)
    return (jnp.stack(bases), jnp.stack(factors))
```

```python
import math

import jax
import jax.numpy as jnp
from jax import lax
from jax.experimental import pallas as pl
from jax.experimental.pallas import tpu as pltpu
from jax.sharding import PartitionSpec as P

MESH = pl.DeviceIdType.MESH
HIGHEST = lax.Precision.HIGHEST
f32, bf16 = jnp.float32, jnp.bfloat16
NN = (((1,), (0,)), ((), ()))
NT = (((1,), (1,)), ((), ()))


def dot(a, b, dims, precision=None):
    return lax.dot_general(a, b, dims, precision=precision, preferred_element_type=f32)


def halves(value):
    high = value.astype(bf16)
    low = (value - high.astype(f32)).astype(bf16)
    return jnp.concatenate([high, low], axis=0)


def fold(value):
    rows = value.shape[0] // 2
    return value[:rows] + value[rows:]


def inverse_factor(gram):
    n = gram.shape[0]
    rows = lax.broadcasted_iota(jnp.int32, (n, n), 0)
    cols = lax.broadcasted_iota(jnp.int32, (n, n), 1)
    left, right = gram, jnp.where(rows == cols, 1.0, 0.0).astype(f32)
    for j in range(n - 1):
        factor = left[:, j : j + 1] / left[j : j + 1, j : j + 1]
        factor = jnp.where(rows > j, factor, 0.0)
        left, right = left - factor * left[j : j + 1, :], right - factor * right[j : j + 1, :]
    pivots = jnp.sum(jnp.where(rows == cols, left, 0.0), axis=1, keepdims=True)
    return right / jnp.sqrt(pivots)


def wait_bytes(ref, sem):
    pltpu.make_async_copy(ref, ref, sem).wait()


def kernel(
    t0_in, t1_in, g_in, f_in, s_in, rb_out, cf_out,
    t0, t1, g, f, s, u, u_got, g_got, part, rsb, zbuf, pfull, mpart, rs2b, acc2, z2b, mfull, linv, rb, cf,
    load_sem, store_sem, u_sem, g_sem, rs_send, rs_recv, z_sem, ag_send, ag_recv, rs2_sem, z2_sem, ag2_sem,
):
    rem, div = lax.rem, lax.div
    dp, c, gen = lax.axis_index("dp"), lax.axis_index("mp"), lax.axis_index("gen")
    x, y, zlo = div(dp, 32), rem(dp, 4), rem(div(dp, 4), 8)
    z = gen * 8 + zlo
    me = x * 4 + y

    def device(x2, y2, z2, c2):
        return (x2 * 32 + rem(z2, 8) * 4 + y2, c2, div(z2, 8))

    partner = device(x, y, rem(z + 8, 16), c)

    def z_step(i):
        h = div(i + 1, 2)
        return 8 + h * (1 - 2 * rem(i, 2))

    def xy_step(i):
        return rem(2 + div(i, 4), 4), rem(2 + i, 4)

    def loop(n, body):
        def step(i, carry):
            body(i)
            return carry

        lax.fori_loop(0, n, step, 0)

    barrier = pltpu.get_barrier_semaphore()

    def hello_z(i):
        pl.semaphore_signal(
            barrier, inc=1, device_id=device(x, y, rem(z + z_step(i), 16), c), device_id_type=MESH
        )

    def hello_xy(i):
        dx, dy = xy_step(div(i, 2))
        dc = rem(i, 2)

        @pl.when(dx + dy + dc != 0)
        def _():
            pl.semaphore_signal(
                barrier, inc=1,
                device_id=device(rem(x + dx, 4), rem(y + dy, 4), z, rem(c + dc, 2)), device_id_type=MESH,
            )

    loads = [
        pltpu.make_async_copy(s_in, s, load_sem.at[0]),
        pltpu.make_async_copy(g_in.at[0], g.at[0], load_sem.at[1]),
        pltpu.make_async_copy(g_in.at[1], g.at[1], load_sem.at[2]),
        pltpu.make_async_copy(t1_in, t1, load_sem.at[3]),
        pltpu.make_async_copy(f_in.at[1], f.at[1], load_sem.at[4]),
        pltpu.make_async_copy(f_in.at[0], f.at[0], load_sem.at[5]),
        pltpu.make_async_copy(t0_in, t0, load_sem.at[6]),
    ]
    loop(15, hello_z)
    for load in loads:
        load.start()
    loop(32, hello_xy)

    loads[0].wait()
    loads[1].wait()
    u_all = dot(s[0], g[0], NT)
    u[0] = u_all[:, :128]
    u[1] = u_all[:, 128:]
    loads[2].wait()
    u1 = halves(dot(s[1], g[1], NT))
    loads[3].wait()
    loads[4].wait()
    for q in range(4):
        span = slice(384 * q, 384 * q + 384)
        block = fold(dot(u1, t1[:, span], NN)) + dot(s[1], f[1, span, :], NT)
        part[1, 4 * q : 4 * q + 4] = block.reshape(4, 8, 384)
    loads[5].wait()
    for q in range(4):
        span = slice(384 * q, 384 * q + 384)
        part[0, 4 * q : 4 * q + 4] = dot(s[0], f[0, span, :], NT).reshape(4, 8, 384)

    pl.semaphore_wait(barrier, 46)

    u_copy = pltpu.make_async_remote_copy(
        src_ref=u.at[1 - gen], dst_ref=u_got, send_sem=u_sem.at[0], recv_sem=u_sem.at[1],
        device_id=partner, device_id_type=MESH,
    )
    u_copy.start()

    def send_part(layer):
        def body(i):
            dx, dy = xy_step(i)
            x2, y2 = rem(x + dx, 4), rem(y + dy, 4)
            slot = (dx * 4 + dy) * 2 + rem(c + layer, 2)

            @pl.when(slot != 0)
            def _():
                pltpu.make_async_remote_copy(
                    src_ref=part.at[layer, x2 * 4 + y2], dst_ref=rsb.at[slot],
                    send_sem=rs_send.at[layer], recv_sem=rs_recv,
                    device_id=device(x2, y2, z, layer), device_id_type=MESH,
                ).start()

        loop(16, body)

    def reduce_part(layer):
        wait_bytes(rsb.at[pl.ds(1, 31)], rs_recv)
        total = part[layer, me]
        for slot in range(1, 32):
            total = total + rsb[slot]
        zbuf[z] = total

        def body(i):
            pltpu.make_async_remote_copy(
                src_ref=zbuf.at[z], dst_ref=zbuf.at[z], send_sem=z_sem.at[0], recv_sem=z_sem.at[1],
                device_id=device(x, y, rem(z + z_step(i), 16), c), device_id_type=MESH,
            ).start()

        loop(15, body)

    def gather_power(layer):
        wait_bytes(zbuf.at[pl.ds(0, 15)], z_sem.at[1])
        total = zbuf[0]
        for slot in range(1, 16):
            total = total + zbuf[slot]
        pfull[layer, me] = total

        def body(i):
            dx, dy = xy_step(div(i, 2))
            dc = rem(i, 2)

            @pl.when(dx + dy + dc != 0)
            def _():
                pltpu.make_async_remote_copy(
                    src_ref=pfull.at[layer, me], dst_ref=pfull.at[layer, me],
                    send_sem=ag_send, recv_sem=ag_recv.at[layer],
                    device_id=device(rem(x + dx, 4), rem(y + dy, 4), z, rem(c + dc, 2)), device_id_type=MESH,
                ).start()

        loop(32, body)

    def wait_power(layer):
        @pl.when(c == layer)
        def _():
            wait_bytes(pfull.at[layer, pl.ds(0, 15)], ag_recv.at[layer])

        @pl.when(c != layer)
        def _():
            wait_bytes(pfull.at[layer, pl.ds(0, 16)], ag_recv.at[layer])

    def power_block(layer, q):
        return pfull[layer, 4 * q : 4 * q + 4].reshape(32, 384)

    send_part(1)
    g_copy = pltpu.make_async_remote_copy(
        src_ref=g.at[0, pl.ds(pl.multiple_of((1 - gen) * 128, 128), 128)], dst_ref=g_got,
        send_sem=g_sem.at[0], recv_sem=g_sem.at[1], device_id=partner, device_id_type=MESH,
    )
    g_copy.start()

    @pl.when(c == 1)
    def _():
        reduce_part(1)

    loads[6].wait()
    u_copy.wait()
    u0 = halves(u[gen] + u_got[...])
    for q in range(4):
        span = slice(384 * q, 384 * q + 384)
        block = fold(dot(u0, t0[:, span], NN)).reshape(4, 8, 384)
        part[0, 4 * q : 4 * q + 4] = part[0, 4 * q : 4 * q + 4] + block
    send_part(0)

    @pl.when(c == 1)
    def _():
        gather_power(1)

    @pl.when(c == 0)
    def _():
        reduce_part(0)
        gather_power(0)

    def products(layer, tokens):
        direct, by_token = None, None
        for q in range(4):
            span = slice(384 * q, 384 * q + 384)
            block = halves(power_block(layer, q))
            one = dot(block, f[layer, span, :], NN)
            two = dot(block, tokens[:, span], NT)
            direct = one if direct is None else direct + one
            by_token = two if by_token is None else by_token + two
        return fold(direct), halves(fold(by_token))

    def put(place, value):
        for q in range(3):
            mpart[4 * q : 4 * q + 4, place] = value[:, 128 * q : 128 * q + 128].reshape(4, 8, 128)

    def factorize(layer):
        gram = None
        for q in range(4):
            block = power_block(layer, q)
            one = dot(block, block, NT, HIGHEST)
            gram = one if gram is None else gram + one
        inverse = inverse_factor(gram)
        linv[layer] = inverse
        scaled = inverse * math.sqrt(1536)
        for q in range(4):
            rb[layer, :, 384 * q : 384 * q + 384] = dot(scaled, power_block(layer, q), NN, HIGHEST)

    rb_stores = [pltpu.make_async_copy(rb.at[i], rb_out.at[i], store_sem.at[i]) for i in range(2)]

    wait_power(1)
    direct, by_token = products(1, t1)
    put(1, direct + fold(dot(by_token, g[1], NN)))
    factorize(1)
    rb_stores[1].start()

    g_copy.wait()
    wait_power(0)
    direct, by_token = products(0, t0)
    own_rows = g[0, pl.ds(pl.multiple_of(gen * 128, 128), 128), :]
    put(0, direct + fold(dot(by_token, own_rows, NN)))
    put(2, fold(dot(by_token, g_got[...], NN)))

    def send_coeffs(i):
        dx, dy = xy_step(i)
        x2, y2 = rem(x + dx, 4), rem(y + dy, 4)

        @pl.when((dx + dy != 0) & (x2 < 3))
        def _():
            pltpu.make_async_remote_copy(
                src_ref=mpart.at[x2 * 4 + y2], dst_ref=rs2b.at[dx * 4 + dy],
                send_sem=rs2_sem.at[0], recv_sem=rs2_sem.at[1],
                device_id=device(x2, y2, z, c), device_id_type=MESH,
            ).start()

    loop(16, send_coeffs)
    factorize(0)
    rb_stores[0].start()

    @pl.when(x < 3)
    def _():
        wait_bytes(rs2b.at[pl.ds(1, 15)], rs2_sem.at[1])
        total = mpart[me]
        for slot in range(1, 16):
            total = total + rs2b[slot]
        acc2[...] = total
        z2b[z] = total[:2]

        def body(i):
            z2 = rem(z + z_step(i), 16)
            where = device(x, y, z2, c)

            @pl.when(div(z2, 8) == gen)
            def _():
                pltpu.make_async_remote_copy(
                    src_ref=acc2.at[pl.ds(0, 2)], dst_ref=z2b.at[z],
                    send_sem=z2_sem.at[0], recv_sem=z2_sem.at[1], device_id=where, device_id_type=MESH,
                ).start()

            @pl.when(div(z2, 8) != gen)
            def _():
                pltpu.make_async_remote_copy(
                    src_ref=acc2.at[2], dst_ref=z2b.at[z, 0],
                    send_sem=z2_sem.at[2], recv_sem=z2_sem.at[3], device_id=where, device_id_type=MESH,
                ).start()

        loop(15, body)
        wait_bytes(z2b.at[pl.ds(0, 7)], z2_sem.at[1])
        wait_bytes(z2b.at[pl.ds(0, 4)], z2_sem.at[3])
        first = z2b[0, 0]
        for slot in range(1, 16):
            first = first + z2b[slot, 0]
        second = z2b[gen * 8, 1]
        for slot in range(1, 8):
            second = second + z2b[gen * 8 + slot, 1]
        mfull[me, 0] = first
        mfull[me, 1] = second

        def share(i):
            dx, dy = xy_step(i)

            @pl.when(dx + dy != 0)
            def _():
                pltpu.make_async_remote_copy(
                    src_ref=mfull.at[me], dst_ref=mfull.at[me],
                    send_sem=ag2_sem.at[0], recv_sem=ag2_sem.at[1],
                    device_id=device(rem(x + dx, 4), rem(y + dy, 4), z, c), device_id_type=MESH,
                ).start()

        loop(16, share)
        wait_bytes(mfull.at[pl.ds(0, 11)], ag2_sem.at[1])

    @pl.when(x == 3)
    def _():
        wait_bytes(mfull.at[pl.ds(0, 12)], ag2_sem.at[1])

    for layer in range(2):
        scaled = linv[layer] * (1.0 / 128.0)
        for q in range(3):
            block = mfull[4 * q : 4 * q + 4, layer].reshape(32, 128)
            cf[layer, :, 128 * q : 128 * q + 128] = dot(scaled, block, NN, HIGHEST)
    cf_store = pltpu.make_async_copy(cf, cf_out, store_sem.at[2])
    cf_store.start()

    for layer in range(2):

        @pl.when(c == layer)
        def _():
            wait_bytes(part.at[layer, pl.ds(0, 15)], rs_send.at[layer])

        @pl.when(c != layer)
        def _():
            wait_bytes(part.at[layer, pl.ds(0, 16)], rs_send.at[layer])

    wait_bytes(zbuf.at[pl.ds(0, 15)], z_sem.at[0])
    wait_bytes(rsb.at[pl.ds(0, 31)], ag_send)

    @pl.when(x < 3)
    def _():
        wait_bytes(mpart.at[pl.ds(0, 11)], rs2_sem.at[0])
        wait_bytes(z2b.at[pl.ds(0, 7)], z2_sem.at[0])
        wait_bytes(z2b.at[pl.ds(0, 4)], z2_sem.at[2])
        wait_bytes(rs2b.at[pl.ds(0, 10)], ag2_sem.at[0])

    @pl.when(x == 3)
    def _():
        wait_bytes(mpart.at[pl.ds(0, 12)], rs2_sem.at[0])

    rb_stores[0].wait()
    rb_stores[1].wait()
    cf_store.wait()


def local(fresh_tokens, saved_tokens, cotangents, feedback, start_factors):
    anywhere = pl.BlockSpec(memory_space=pl.ANY)
    vmem, dma = pltpu.VMEM, pltpu.SemaphoreType.DMA
    rb, cf = pl.pallas_call(
        kernel,
        out_shape=(
            jax.ShapeDtypeStruct((2, 32, 1536), f32),
            jax.ShapeDtypeStruct((2, 32, 384), f32),
        ),
        in_specs=[anywhere] * 5,
        out_specs=(anywhere, anywhere),
        scratch_shapes=[
            vmem((128, 1536), bf16),
            vmem((256, 1536), bf16),
            vmem((2, 256, 384), bf16),
            vmem((2, 1536, 384), bf16),
            vmem((2, 32, 384), bf16),
            vmem((2, 32, 128), f32),
            vmem((32, 128), f32),
            vmem((128, 384), bf16),
            vmem((2, 16, 8, 384), f32),
            vmem((32, 8, 384), f32),
            vmem((16, 8, 384), f32),
            vmem((2, 16, 8, 384), f32),
            vmem((12, 3, 8, 128), f32),
            vmem((16, 3, 8, 128), f32),
            vmem((3, 8, 128), f32),
            vmem((16, 2, 8, 128), f32),
            vmem((12, 2, 8, 128), f32),
            vmem((2, 32, 32), f32),
            vmem((2, 32, 1536), f32),
            vmem((2, 32, 384), f32),
            dma((7,)),
            dma((3,)),
            dma((2,)),
            dma((2,)),
            dma((2,)),
            dma,
            dma((2,)),
            dma,
            dma((2,)),
            dma((2,)),
            dma((4,)),
            dma((2,)),
        ],
        compiler_params=pltpu.CompilerParams(
            collective_id=0, has_side_effects=True, vmem_limit_bytes=60 * 2**20
        ),
        cost_estimate=pl.CostEstimate(flops=10**9, bytes_accessed=5 * 10**6, transcendentals=0),
        name="compress",
    )(
        fresh_tokens,
        saved_tokens,
        cotangents,
        feedback.reshape(2, 1536, 384),
        jnp.transpose(start_factors, (0, 2, 1)),
    )
    return jnp.transpose(rb, (0, 2, 1)), jnp.transpose(cf, (0, 2, 1))


def solution(mesh):
    return jax.shard_map(
        local,
        mesh=mesh,
        in_specs=(
            P(("dp", "gen"), None),
            P("dp", None),
            P(None, "dp", ("mp", "gen")),
            P(None, "dp", None, ("mp", "gen")),
            P(None, ("mp", "gen"), None),
        ),
        out_specs=(P(), P(None, ("mp", "gen"), None)),
        check_vma=False,
    )
```

```python
import math

import jax
import jax.numpy as jnp
from jax import lax
from jax.experimental import pallas as pl
from jax.experimental.pallas import tpu as pltpu
from jax.sharding import PartitionSpec as P

MESH = pl.DeviceIdType.MESH
HIGHEST = lax.Precision.HIGHEST
f32, bf16 = jnp.float32, jnp.bfloat16
NN = (((1,), (0,)), ((), ()))
NT = (((1,), (1,)), ((), ()))
XY_STEPS = sorted(
    [(dx, dy) for dx in range(4) for dy in range(4) if dx + dy > 0],
    key=lambda step: -sum(min(d, 4 - d) for d in step),
)
Z_STEPS = sorted(range(1, 16), key=lambda d: -min(d, 16 - d))


def dot(a, b, dims, precision=None):
    return lax.dot_general(a, b, dims, precision=precision, preferred_element_type=f32)


def halves(value):
    high = value.astype(bf16)
    low = (value - high.astype(f32)).astype(bf16)
    return jnp.concatenate([high, low], axis=0)


def fold(value):
    rows = value.shape[0] // 2
    return value[:rows] + value[rows:]


def inverse_factor(gram):
    n = gram.shape[0]
    rows = lax.broadcasted_iota(jnp.int32, (n, n), 0)
    cols = lax.broadcasted_iota(jnp.int32, (n, n), 1)
    left, right = gram, jnp.where(rows == cols, 1.0, 0.0).astype(f32)
    for j in range(n - 1):
        factor = left[:, j : j + 1] / left[j : j + 1, j : j + 1]
        factor = jnp.where(rows > j, factor, 0.0)
        left, right = left - factor * left[j : j + 1, :], right - factor * right[j : j + 1, :]
    pivots = jnp.sum(jnp.where(rows == cols, left, 0.0), axis=1, keepdims=True)
    return right / jnp.sqrt(pivots)


def wait_bytes(ref, sem):
    pltpu.make_async_copy(ref, ref, sem).wait()


def kernel(
    t0_in, t1_in, g_in, f_in, s_in, rb_out, cf_out,
    t0, t1, g, f, s, u, u_got, g_got, part, rsb, zbuf, pfull, mpart, rs2b, acc2, z2b, mfull, linv, rb, cf,
    load_sem, store_sem, u_sem, g_sem, rs_send, rs_recv, z_sem, ag_send, ag_recv, rs2_sem, z2_sem, ag2_sem,
):
    rem, div = lax.rem, lax.div
    dp, c, gen = lax.axis_index("dp"), lax.axis_index("mp"), lax.axis_index("gen")
    x, y, zlo = div(dp, 32), rem(dp, 4), rem(div(dp, 4), 8)
    z = gen * 8 + zlo
    me = x * 4 + y
    xs = [x] + [rem(x + d, 4) for d in range(1, 4)]
    ys = [y] + [rem(y + d, 4) for d in range(1, 4)]
    cs = [c, 1 - c]
    column = zlo * 4

    def plane(dx, dy, core):
        return (xs[dx] * 32 + column + ys[dy], core, gen)

    def along(dz):
        other = rem(z + dz, 16)
        return (x * 32 + rem(other, 8) * 4 + y, c, div(other, 8))

    partner = (dp, c, 1 - gen)

    def send(src, dst, send_sem, recv_sem, device):
        pltpu.make_async_remote_copy(
            src_ref=src, dst_ref=dst, send_sem=send_sem, recv_sem=recv_sem,
            device_id=device, device_id_type=MESH,
        ).start()

    loads = [
        pltpu.make_async_copy(s_in, s, load_sem.at[0]),
        pltpu.make_async_copy(g_in.at[0], g.at[0], load_sem.at[1]),
        pltpu.make_async_copy(g_in.at[1], g.at[1], load_sem.at[2]),
        pltpu.make_async_copy(t1_in, t1, load_sem.at[3]),
        pltpu.make_async_copy(f_in.at[1], f.at[1], load_sem.at[4]),
        pltpu.make_async_copy(f_in.at[0], f.at[0], load_sem.at[5]),
        pltpu.make_async_copy(t0_in, t0, load_sem.at[6]),
    ]
    for load in loads:
        load.start()

    barrier = pltpu.get_barrier_semaphore()
    peers = [along(dz) for dz in Z_STEPS] + [plane(*step, cs[k]) for step in XY_STEPS for k in range(2)]
    for peer in peers + [plane(0, 0, cs[1])]:
        pl.semaphore_signal(barrier, inc=1, device_id=peer, device_id_type=MESH)

    loads[0].wait()
    loads[1].wait()
    u_all = dot(s[0], g[0], NT)
    u[0] = u_all[:, :128]
    u[1] = u_all[:, 128:]
    u_copy = pltpu.make_async_remote_copy(
        src_ref=u.at[1 - gen], dst_ref=u_got, send_sem=u_sem.at[0], recv_sem=u_sem.at[1],
        device_id=partner, device_id_type=MESH,
    )

    g_copy = pltpu.make_async_remote_copy(
        src_ref=g.at[0, pl.ds(pl.multiple_of((1 - gen) * 128, 128), 128)], dst_ref=g_got,
        send_sem=g_sem.at[0], recv_sem=g_sem.at[1], device_id=partner, device_id_type=MESH,
    )

    @pl.when(gen == 1)
    def _():
        pl.semaphore_wait(barrier, 46)
        u_copy.start()
        g_copy.start()

    loads[2].wait()
    u1 = halves(dot(s[1], g[1], NT))
    loads[3].wait()
    loads[4].wait()
    for q in range(4):
        span = slice(384 * q, 384 * q + 384)
        block = fold(dot(u1, t1[:, span], NN)) + dot(s[1], f[1, span, :], NT)
        part[1, 4 * q : 4 * q + 4] = block.reshape(4, 8, 384)
    loads[5].wait()
    for q in range(4):
        span = slice(384 * q, 384 * q + 384)
        part[0, 4 * q : 4 * q + 4] = dot(s[0], f[0, span, :], NT).reshape(4, 8, 384)
    loads[6].wait()

    @pl.when(gen == 0)
    def _():
        pl.semaphore_wait(barrier, 46)
        u_copy.start()
        g_copy.start()

    def send_part(layer):
        other = rem(c + layer, 2)
        for dx, dy in XY_STEPS:
            send(
                part.at[layer, xs[dx] * 4 + ys[dy]], rsb.at[(dx * 4 + dy) * 2 + other],
                rs_send.at[layer], rs_recv, plane(dx, dy, layer),
            )

        @pl.when(other == 1)
        def _():
            send(part.at[layer, me], rsb.at[1], rs_send.at[layer], rs_recv, plane(0, 0, layer))

    def reduce_part(layer):
        wait_bytes(rsb.at[pl.ds(1, 31)], rs_recv)
        total = part[layer, me]
        for slot in range(1, 32):
            total = total + rsb[slot]
        zbuf[z] = total
        for dz in Z_STEPS:
            send(zbuf.at[z], zbuf.at[z], z_sem.at[0], z_sem.at[1], along(dz))

    def gather_power(layer):
        wait_bytes(zbuf.at[pl.ds(0, 15)], z_sem.at[1])
        total = zbuf[0]
        for slot in range(1, 16):
            total = total + zbuf[slot]
        pfull[layer, me] = total
        for dx, dy in XY_STEPS + [(0, 0)]:
            for k in range(2):
                if dx + dy + k > 0:
                    send(
                        pfull.at[layer, me], pfull.at[layer, me],
                        ag_send, ag_recv.at[layer], plane(dx, dy, cs[k]),
                    )

    def wait_power(layer):
        @pl.when(c == layer)
        def _():
            wait_bytes(pfull.at[layer, pl.ds(0, 15)], ag_recv.at[layer])

        @pl.when(c != layer)
        def _():
            wait_bytes(pfull.at[layer, pl.ds(0, 16)], ag_recv.at[layer])

    def power_block(layer, q):
        return pfull[layer, 4 * q : 4 * q + 4].reshape(32, 384)

    send_part(1)

    @pl.when((c == 1) & (gen == 1))
    def _():
        reduce_part(1)

    u_copy.wait()
    u0 = halves(u[gen] + u_got[...])
    for q in range(4):
        span = slice(384 * q, 384 * q + 384)
        block = fold(dot(u0, t0[:, span], NN)).reshape(4, 8, 384)
        part[0, 4 * q : 4 * q + 4] = part[0, 4 * q : 4 * q + 4] + block
    send_part(0)

    @pl.when(c == 1)
    def _():

        @pl.when(gen == 0)
        def _():
            reduce_part(1)

        gather_power(1)

    @pl.when(c == 0)
    def _():
        reduce_part(0)
        gather_power(0)

    def products(layer, tokens):
        direct, by_token = None, None
        for q in range(4):
            span = slice(384 * q, 384 * q + 384)
            block = halves(power_block(layer, q))
            one = dot(block, f[layer, span, :], NN)
            two = dot(block, tokens[:, span], NT)
            direct = one if direct is None else direct + one
            by_token = two if by_token is None else by_token + two
        return fold(direct), halves(fold(by_token))

    def put(place, value):
        for q in range(3):
            mpart[4 * q : 4 * q + 4, place] = value[:, 128 * q : 128 * q + 128].reshape(4, 8, 128)

    def factorize(layer):
        gram = None
        for q in range(4):
            block = power_block(layer, q)
            one = dot(block, block, NT, HIGHEST)
            gram = one if gram is None else gram + one
        inverse = inverse_factor(gram)
        linv[layer] = inverse
        scaled = inverse * math.sqrt(1536)
        for q in range(4):
            rb[layer, :, 384 * q : 384 * q + 384] = dot(scaled, power_block(layer, q), NN, HIGHEST)

    rb_stores = [pltpu.make_async_copy(rb.at[i], rb_out.at[i], store_sem.at[i]) for i in range(2)]

    wait_power(1)
    direct, by_token = products(1, t1)
    put(1, direct + fold(dot(by_token, g[1], NN)))
    factorize(1)
    rb_stores[1].start()

    g_copy.wait()
    wait_power(0)
    direct, by_token = products(0, t0)
    own_rows = g[0, pl.ds(pl.multiple_of(gen * 128, 128), 128), :]
    put(0, direct + fold(dot(by_token, own_rows, NN)))
    put(2, fold(dot(by_token, g_got[...], NN)))

    for dx, dy in XY_STEPS:

        @pl.when(xs[dx] < 3)
        def _():
            send(
                mpart.at[xs[dx] * 4 + ys[dy]], rs2b.at[dx * 4 + dy],
                rs2_sem.at[0], rs2_sem.at[1], plane(dx, dy, c),
            )

    factorize(0)
    rb_stores[0].start()

    @pl.when(x < 3)
    def _():
        wait_bytes(rs2b.at[pl.ds(1, 15)], rs2_sem.at[1])
        total = mpart[me]
        for slot in range(1, 16):
            total = total + rs2b[slot]
        acc2[...] = total
        z2b[z] = total[:2]

        for dz in Z_STEPS:
            where = along(dz)

            @pl.when(where[2] == gen)
            def _():
                send(acc2.at[pl.ds(0, 2)], z2b.at[z], z2_sem.at[0], z2_sem.at[1], where)

            @pl.when(where[2] != gen)
            def _():
                send(acc2.at[2], z2b.at[z, 0], z2_sem.at[2], z2_sem.at[3], where)

        wait_bytes(z2b.at[pl.ds(0, 7)], z2_sem.at[1])
        wait_bytes(z2b.at[pl.ds(0, 4)], z2_sem.at[3])
        first = z2b[0, 0]
        for slot in range(1, 16):
            first = first + z2b[slot, 0]
        second = z2b[gen * 8, 1]
        for slot in range(1, 8):
            second = second + z2b[gen * 8 + slot, 1]
        mfull[me, 0] = first
        mfull[me, 1] = second

        for step in XY_STEPS:
            send(mfull.at[me], mfull.at[me], ag2_sem.at[0], ag2_sem.at[1], plane(*step, c))
        wait_bytes(mfull.at[pl.ds(0, 11)], ag2_sem.at[1])

    @pl.when(x == 3)
    def _():
        wait_bytes(mfull.at[pl.ds(0, 12)], ag2_sem.at[1])

    for layer in range(2):
        scaled = linv[layer] * (1.0 / 128.0)
        for q in range(3):
            block = mfull[4 * q : 4 * q + 4, layer].reshape(32, 128)
            cf[layer, :, 128 * q : 128 * q + 128] = dot(scaled, block, NN, HIGHEST)
    cf_store = pltpu.make_async_copy(cf, cf_out, store_sem.at[2])
    cf_store.start()

    for layer in range(2):

        @pl.when(c == layer)
        def _():
            wait_bytes(part.at[layer, pl.ds(0, 15)], rs_send.at[layer])

        @pl.when(c != layer)
        def _():
            wait_bytes(part.at[layer, pl.ds(0, 16)], rs_send.at[layer])

    wait_bytes(zbuf.at[pl.ds(0, 15)], z_sem.at[0])
    wait_bytes(rsb.at[pl.ds(0, 31)], ag_send)

    @pl.when(x < 3)
    def _():
        wait_bytes(mpart.at[pl.ds(0, 11)], rs2_sem.at[0])
        wait_bytes(z2b.at[pl.ds(0, 7)], z2_sem.at[0])
        wait_bytes(z2b.at[pl.ds(0, 4)], z2_sem.at[2])
        wait_bytes(rs2b.at[pl.ds(0, 10)], ag2_sem.at[0])

    @pl.when(x == 3)
    def _():
        wait_bytes(mpart.at[pl.ds(0, 12)], rs2_sem.at[0])

    rb_stores[0].wait()
    rb_stores[1].wait()
    cf_store.wait()


def write_out(rb, cf, rb_out, cf_out, sem):
    copies = [
        pltpu.make_async_copy(rb, rb_out, sem.at[0]),
        pltpu.make_async_copy(cf, cf_out, sem.at[1]),
    ]
    for copy in copies:
        copy.start()
    for copy in copies:
        copy.wait()


def local(fresh_tokens, saved_tokens, cotangents, feedback, start_factors):
    anywhere = pl.BlockSpec(memory_space=pl.ANY)
    vmem, dma = pltpu.VMEM, pltpu.SemaphoreType.DMA
    rb, cf = pl.pallas_call(
        kernel,
        out_shape=(
            jax.ShapeDtypeStruct((2, 32, 1536), f32),
            jax.ShapeDtypeStruct((2, 32, 384), f32),
        ),
        in_specs=[anywhere] * 5,
        out_specs=(anywhere, anywhere),
        scratch_shapes=[
            vmem((128, 1536), bf16),
            vmem((256, 1536), bf16),
            vmem((2, 256, 384), bf16),
            vmem((2, 1536, 384), bf16),
            vmem((2, 32, 384), bf16),
            vmem((2, 32, 128), f32),
            vmem((32, 128), f32),
            vmem((128, 384), bf16),
            vmem((2, 16, 8, 384), f32),
            vmem((32, 8, 384), f32),
            vmem((16, 8, 384), f32),
            vmem((2, 16, 8, 384), f32),
            vmem((12, 3, 8, 128), f32),
            vmem((16, 3, 8, 128), f32),
            vmem((3, 8, 128), f32),
            vmem((16, 2, 8, 128), f32),
            vmem((12, 2, 8, 128), f32),
            vmem((2, 32, 32), f32),
            vmem((2, 32, 1536), f32),
            vmem((2, 32, 384), f32),
            dma((7,)),
            dma((3,)),
            dma((2,)),
            dma((2,)),
            dma((2,)),
            dma,
            dma((2,)),
            dma,
            dma((2,)),
            dma((2,)),
            dma((4,)),
            dma((2,)),
        ],
        compiler_params=pltpu.CompilerParams(
            collective_id=0, has_side_effects=True, vmem_limit_bytes=60 * 2**20
        ),
        cost_estimate=pl.CostEstimate(flops=10**9, bytes_accessed=5 * 10**6, transcendentals=0),
        name="compress",
    )(
        fresh_tokens,
        saved_tokens,
        cotangents,
        feedback.reshape(2, 1536, 384),
        jnp.transpose(start_factors, (0, 2, 1)),
    )
    rb, cf = pl.pallas_call(
        write_out,
        out_shape=(
            jax.ShapeDtypeStruct((2, 32, 1536), f32),
            jax.ShapeDtypeStruct((2, 32, 384), f32),
        ),
        in_specs=[pl.BlockSpec(memory_space=vmem)] * 2,
        out_specs=(anywhere, anywhere),
        scratch_shapes=[dma((2,))],
        name="write_out",
    )(rb, cf)
    return jnp.transpose(rb, (0, 2, 1)), jnp.transpose(cf, (0, 2, 1))


def solution(mesh):
    return jax.shard_map(
        local,
        mesh=mesh,
        in_specs=(
            P(("dp", "gen"), None),
            P("dp", None),
            P(None, "dp", ("mp", "gen")),
            P(None, "dp", None, ("mp", "gen")),
            P(None, ("mp", "gen"), None),
        ),
        out_specs=(P(), P(None, ("mp", "gen"), None)),
        check_vma=False,
    )
```

```python
import math

import jax
import jax.numpy as jnp
from jax import lax
from jax.experimental import pallas as pl
from jax.experimental.pallas import tpu as pltpu
from jax.sharding import PartitionSpec as P

MESH = pl.DeviceIdType.MESH
HIGHEST = lax.Precision.HIGHEST
f32, bf16 = jnp.float32, jnp.bfloat16
NN = (((1,), (0,)), ((), ()))
NT = (((1,), (1,)), ((), ()))
XY_STEPS = sorted(
    [(dx, dy) for dx in range(4) for dy in range(4) if dx + dy > 0],
    key=lambda step: -sum(min(d, 4 - d) for d in step),
)
Z_STEPS = sorted(range(1, 16), key=lambda d: -min(d, 16 - d))


def dot(a, b, dims, precision=None):
    return lax.dot_general(a, b, dims, precision=precision, preferred_element_type=f32)


def halves(value):
    high = value.astype(bf16)
    low = (value - high.astype(f32)).astype(bf16)
    return jnp.concatenate([high, low], axis=0)


def fold(value):
    rows = value.shape[0] // 2
    return value[:rows] + value[rows:]


def inverse_factor(gram):
    n = gram.shape[0]
    rows = lax.broadcasted_iota(jnp.int32, (n, n), 0)
    cols = lax.broadcasted_iota(jnp.int32, (n, n), 1)
    left, right = gram, jnp.where(rows == cols, 1.0, 0.0).astype(f32)
    for j in range(n - 1):
        factor = left[:, j : j + 1] / left[j : j + 1, j : j + 1]
        factor = jnp.where(rows > j, factor, 0.0)
        left, right = left - factor * left[j : j + 1, :], right - factor * right[j : j + 1, :]
    pivots = jnp.sum(jnp.where(rows == cols, left, 0.0), axis=1, keepdims=True)
    return right / jnp.sqrt(pivots)


def wait_bytes(ref, sem):
    pltpu.make_async_copy(ref, ref, sem).wait()


def kernel(
    t0_in, t1_in, g_in, f_in, s_in, rb_out, m_out, linv_out,
    t0, t1, g, f, s, u, u_got, g_got, part, rsb, zbuf, pfull, mpart, rs2b, acc2, z2b, mine, linv, rb,
    load_sem, store_sem, u_sem, g_sem, rs_send, rs_recv, z_sem, ag_send, ag_recv, rs2_sem, z2_sem, ag2_sem,
):
    rem, div = lax.rem, lax.div
    dp, c, gen = lax.axis_index("dp"), lax.axis_index("mp"), lax.axis_index("gen")
    x, y, zlo = div(dp, 32), rem(dp, 4), rem(div(dp, 4), 8)
    z = gen * 8 + zlo
    me = x * 4 + y
    xs = [x] + [rem(x + d, 4) for d in range(1, 4)]
    ys = [y] + [rem(y + d, 4) for d in range(1, 4)]
    cs = [c, 1 - c]
    column = zlo * 4

    def plane(dx, dy, core):
        return (xs[dx] * 32 + column + ys[dy], core, gen)

    def along(dz):
        other = rem(z + dz, 16)
        return (x * 32 + rem(other, 8) * 4 + y, c, div(other, 8))

    partner = (dp, c, 1 - gen)

    def send(src, dst, send_sem, recv_sem, device):
        pltpu.make_async_remote_copy(
            src_ref=src, dst_ref=dst, send_sem=send_sem, recv_sem=recv_sem,
            device_id=device, device_id_type=MESH,
        ).start()

    loads = [
        pltpu.make_async_copy(s_in, s, load_sem.at[0]),
        pltpu.make_async_copy(g_in.at[0], g.at[0], load_sem.at[1]),
        pltpu.make_async_copy(g_in.at[1], g.at[1], load_sem.at[2]),
        pltpu.make_async_copy(t1_in, t1, load_sem.at[3]),
        pltpu.make_async_copy(f_in.at[1], f.at[1], load_sem.at[4]),
        pltpu.make_async_copy(f_in.at[0], f.at[0], load_sem.at[5]),
        pltpu.make_async_copy(t0_in, t0, load_sem.at[6]),
    ]
    for load in loads:
        load.start()

    barrier = pltpu.get_barrier_semaphore()
    peers = [along(dz) for dz in Z_STEPS] + [plane(*step, cs[k]) for step in XY_STEPS for k in range(2)]
    for peer in peers + [plane(0, 0, cs[1])]:
        pl.semaphore_signal(barrier, inc=1, device_id=peer, device_id_type=MESH)

    loads[0].wait()
    loads[1].wait()
    u_all = dot(s[0], g[0], NT)
    u[0] = u_all[:, :128]
    u[1] = u_all[:, 128:]
    u_copy = pltpu.make_async_remote_copy(
        src_ref=u.at[1 - gen], dst_ref=u_got, send_sem=u_sem.at[0], recv_sem=u_sem.at[1],
        device_id=partner, device_id_type=MESH,
    )

    g_copy = pltpu.make_async_remote_copy(
        src_ref=g.at[0, pl.ds(pl.multiple_of((1 - gen) * 128, 128), 128)], dst_ref=g_got,
        send_sem=g_sem.at[0], recv_sem=g_sem.at[1], device_id=partner, device_id_type=MESH,
    )

    @pl.when(gen == 1)
    def _():
        pl.semaphore_wait(barrier, 46)
        u_copy.start()

        @pl.when(c == 0)
        def _():
            g_copy.start()

    loads[2].wait()
    u1 = halves(dot(s[1], g[1], NT))
    loads[3].wait()
    loads[4].wait()
    for q in range(4):
        span = slice(384 * q, 384 * q + 384)
        block = fold(dot(u1, t1[:, span], NN)) + dot(s[1], f[1, span, :], NT)
        part[1, 4 * q : 4 * q + 4] = block.reshape(4, 8, 384)
    loads[5].wait()
    for q in range(4):
        span = slice(384 * q, 384 * q + 384)
        part[0, 4 * q : 4 * q + 4] = dot(s[0], f[0, span, :], NT).reshape(4, 8, 384)
    loads[6].wait()

    @pl.when(gen == 0)
    def _():
        pl.semaphore_wait(barrier, 46)
        u_copy.start()

        @pl.when(c == 0)
        def _():
            g_copy.start()

    def send_part(layer):
        other = rem(c + layer, 2)
        for dx, dy in XY_STEPS:
            send(
                part.at[layer, xs[dx] * 4 + ys[dy]], rsb.at[(dx * 4 + dy) * 2 + other],
                rs_send.at[layer], rs_recv, plane(dx, dy, layer),
            )

        @pl.when(other == 1)
        def _():
            send(part.at[layer, me], rsb.at[1], rs_send.at[layer], rs_recv, plane(0, 0, layer))

    def reduce_part(layer):
        wait_bytes(rsb.at[pl.ds(1, 31)], rs_recv)
        total = part[layer, me]
        for slot in range(1, 32):
            total = total + rsb[slot]
        zbuf[z] = total
        for dz in Z_STEPS:
            send(zbuf.at[z], zbuf.at[z], z_sem.at[0], z_sem.at[1], along(dz))

    def gather_power(layer):
        wait_bytes(zbuf.at[pl.ds(0, 15)], z_sem.at[1])
        total = zbuf[0]
        for slot in range(1, 16):
            total = total + zbuf[slot]
        pfull[layer, me] = total
        for dx, dy in XY_STEPS + [(0, 0)]:
            for k in range(2):
                if dx + dy + k > 0:
                    send(
                        pfull.at[layer, me], pfull.at[layer, me],
                        ag_send, ag_recv.at[layer], plane(dx, dy, cs[k]),
                    )

    def wait_power(layer):
        @pl.when(c == layer)
        def _():
            wait_bytes(pfull.at[layer, pl.ds(0, 15)], ag_recv.at[layer])

        @pl.when(c != layer)
        def _():
            wait_bytes(pfull.at[layer, pl.ds(0, 16)], ag_recv.at[layer])

    def power_block(layer, q):
        return pfull[layer, 4 * q : 4 * q + 4].reshape(32, 384)

    send_part(1)

    @pl.when((c == 1) & (gen == 1))
    def _():
        reduce_part(1)

    u_copy.wait()
    u0 = halves(u[gen] + u_got[...])
    for q in range(4):
        span = slice(384 * q, 384 * q + 384)
        block = fold(dot(u0, t0[:, span], NN)).reshape(4, 8, 384)
        part[0, 4 * q : 4 * q + 4] = part[0, 4 * q : 4 * q + 4] + block
    send_part(0)

    @pl.when(c == 1)
    def _():

        @pl.when(gen == 0)
        def _():
            reduce_part(1)

        g_copy.start()
        gather_power(1)

    @pl.when(c == 0)
    def _():
        reduce_part(0)
        gather_power(0)

    def products(layer, tokens):
        direct, by_token = None, None
        for q in range(4):
            span = slice(384 * q, 384 * q + 384)
            block = halves(power_block(layer, q))
            one = dot(block, f[layer, span, :], NN)
            two = dot(block, tokens[:, span], NT)
            direct = one if direct is None else direct + one
            by_token = two if by_token is None else by_token + two
        return fold(direct), halves(fold(by_token))

    def put(place, value):
        for q in range(3):
            mpart[4 * q : 4 * q + 4, place] = value[:, 128 * q : 128 * q + 128].reshape(4, 8, 128)

    def factorize(layer):
        gram = None
        for q in range(4):
            block = power_block(layer, q)
            one = dot(block, block, NT, HIGHEST)
            gram = one if gram is None else gram + one
        inverse = inverse_factor(gram)
        linv[layer] = inverse
        scaled = inverse * math.sqrt(1536)
        for q in range(4):
            rb[layer, :, 384 * q : 384 * q + 384] = dot(scaled, power_block(layer, q), NN, HIGHEST)

    rb_stores = [pltpu.make_async_copy(rb.at[i], rb_out.at[i], store_sem.at[i]) for i in range(2)]

    wait_power(1)
    direct, by_token = products(1, t1)
    put(1, direct + fold(dot(by_token, g[1], NN)))

    g_copy.wait()
    wait_power(0)
    direct, by_token = products(0, t0)
    own_rows = g[0, pl.ds(pl.multiple_of(gen * 128, 128), 128), :]
    put(0, direct + fold(dot(by_token, own_rows, NN)))
    put(2, fold(dot(by_token, g_got[...], NN)))

    for dx, dy in XY_STEPS:

        @pl.when(xs[dx] < 3)
        def _():
            send(
                mpart.at[xs[dx] * 4 + ys[dy]], rs2b.at[dx * 4 + dy],
                rs2_sem.at[0], rs2_sem.at[1], plane(dx, dy, c),
            )

    factorize(0)
    rb_stores[0].start()

    @pl.when(x < 3)
    def _():
        wait_bytes(rs2b.at[pl.ds(1, 15)], rs2_sem.at[1])
        total = mpart[me]
        for slot in range(1, 16):
            total = total + rs2b[slot]
        acc2[...] = total
        z2b[z] = total[:2]

        for dz in Z_STEPS:
            where = along(dz)

            @pl.when(where[2] == gen)
            def _():
                send(acc2.at[pl.ds(0, 2)], z2b.at[z], z2_sem.at[0], z2_sem.at[1], where)

            @pl.when(where[2] != gen)
            def _():
                send(acc2.at[2], z2b.at[z, 0], z2_sem.at[2], z2_sem.at[3], where)

    factorize(1)
    rb_stores[1].start()
    linv_store = pltpu.make_async_copy(linv, linv_out, store_sem.at[3])
    linv_store.start()

    @pl.when(x < 3)
    def _():
        wait_bytes(z2b.at[pl.ds(0, 7)], z2_sem.at[1])
        wait_bytes(z2b.at[pl.ds(0, 4)], z2_sem.at[3])
        first = z2b[0, 0]
        for slot in range(1, 16):
            first = first + z2b[slot, 0]
        second = z2b[gen * 8, 1]
        for slot in range(1, 8):
            second = second + z2b[gen * 8 + slot, 1]
        mine[0] = first
        mine[1] = second

        for step in XY_STEPS:
            send(mine, m_out.at[me], ag2_sem.at[0], ag2_sem.at[1], plane(*step, c))
        keep = pltpu.make_async_copy(mine, m_out.at[me], store_sem.at[2])
        keep.start()
        wait_bytes(m_out.at[pl.ds(0, 11)], ag2_sem.at[1])
        keep.wait()

    @pl.when(x == 3)
    def _():
        wait_bytes(m_out.at[pl.ds(0, 12)], ag2_sem.at[1])

    for layer in range(2):

        @pl.when(c == layer)
        def _():
            wait_bytes(part.at[layer, pl.ds(0, 15)], rs_send.at[layer])

        @pl.when(c != layer)
        def _():
            wait_bytes(part.at[layer, pl.ds(0, 16)], rs_send.at[layer])

    wait_bytes(zbuf.at[pl.ds(0, 15)], z_sem.at[0])
    wait_bytes(rsb.at[pl.ds(0, 31)], ag_send)

    @pl.when(x < 3)
    def _():
        wait_bytes(mpart.at[pl.ds(0, 11)], rs2_sem.at[0])
        wait_bytes(z2b.at[pl.ds(0, 7)], z2_sem.at[0])
        wait_bytes(z2b.at[pl.ds(0, 4)], z2_sem.at[2])
        wait_bytes(rs2b.at[pl.ds(0, 10)], ag2_sem.at[0])

    @pl.when(x == 3)
    def _():
        wait_bytes(mpart.at[pl.ds(0, 12)], rs2_sem.at[0])

    rb_stores[0].wait()
    rb_stores[1].wait()
    linv_store.wait()


def write_out(rb, sums, inverse, rb_out, cf_out, cf, sem):
    rb_copy = pltpu.make_async_copy(rb, rb_out, sem.at[0])
    rb_copy.start()
    for layer in range(2):
        scaled = inverse[layer] * (1.0 / 128.0)
        for q in range(3):
            block = sums[4 * q : 4 * q + 4, layer].reshape(32, 128)
            cf[layer, :, 128 * q : 128 * q + 128] = dot(scaled, block, NN, HIGHEST)
    cf_copy = pltpu.make_async_copy(cf, cf_out, sem.at[1])
    cf_copy.start()
    rb_copy.wait()
    cf_copy.wait()


def local(fresh_tokens, saved_tokens, cotangents, feedback, start_factors):
    anywhere = pl.BlockSpec(memory_space=pl.ANY)
    vmem, dma = pltpu.VMEM, pltpu.SemaphoreType.DMA
    rb, sums, inverse = pl.pallas_call(
        kernel,
        out_shape=(
            jax.ShapeDtypeStruct((2, 32, 1536), f32),
            jax.ShapeDtypeStruct((12, 2, 8, 128), f32),
            jax.ShapeDtypeStruct((2, 32, 32), f32),
        ),
        in_specs=[anywhere] * 5,
        out_specs=(anywhere, anywhere, anywhere),
        scratch_shapes=[
            vmem((128, 1536), bf16),
            vmem((256, 1536), bf16),
            vmem((2, 256, 384), bf16),
            vmem((2, 1536, 384), bf16),
            vmem((2, 32, 384), bf16),
            vmem((2, 32, 128), f32),
            vmem((32, 128), f32),
            vmem((128, 384), bf16),
            vmem((2, 16, 8, 384), f32),
            vmem((32, 8, 384), f32),
            vmem((16, 8, 384), f32),
            vmem((2, 16, 8, 384), f32),
            vmem((12, 3, 8, 128), f32),
            vmem((16, 3, 8, 128), f32),
            vmem((3, 8, 128), f32),
            vmem((16, 2, 8, 128), f32),
            vmem((2, 8, 128), f32),
            vmem((2, 32, 32), f32),
            vmem((2, 32, 1536), f32),
            dma((7,)),
            dma((4,)),
            dma((2,)),
            dma((2,)),
            dma((2,)),
            dma,
            dma((2,)),
            dma,
            dma((2,)),
            dma((2,)),
            dma((4,)),
            dma((2,)),
        ],
        compiler_params=pltpu.CompilerParams(
            collective_id=0, has_side_effects=True, vmem_limit_bytes=60 * 2**20
        ),
        cost_estimate=pl.CostEstimate(flops=10**9, bytes_accessed=5 * 10**6, transcendentals=0),
        name="compress",
    )(
        fresh_tokens,
        saved_tokens,
        cotangents,
        feedback.reshape(2, 1536, 384),
        jnp.transpose(start_factors, (0, 2, 1)),
    )
    rb, cf = pl.pallas_call(
        write_out,
        out_shape=(
            jax.ShapeDtypeStruct((2, 32, 1536), f32),
            jax.ShapeDtypeStruct((2, 32, 384), f32),
        ),
        in_specs=[pl.BlockSpec(memory_space=vmem)] * 3,
        out_specs=(anywhere, anywhere),
        scratch_shapes=[vmem((2, 32, 384), f32), dma((2,))],
        name="write_out",
    )(rb, sums, inverse)
    return jnp.transpose(rb, (0, 2, 1)), jnp.transpose(cf, (0, 2, 1))


def solution(mesh):
    return jax.shard_map(
        local,
        mesh=mesh,
        in_specs=(
            P(("dp", "gen"), None),
            P("dp", None),
            P(None, "dp", ("mp", "gen")),
            P(None, "dp", None, ("mp", "gen")),
            P(None, ("mp", "gen"), None),
        ),
        out_specs=(P(), P(None, ("mp", "gen"), None)),
        check_vma=False,
    )
```

```python
import math

import jax
import jax.numpy as jnp
from jax import lax
from jax.experimental import pallas as pl
from jax.experimental.pallas import tpu as pltpu
from jax.sharding import PartitionSpec as P

MESH = pl.DeviceIdType.MESH
HIGHEST = lax.Precision.HIGHEST
f32, bf16 = jnp.float32, jnp.bfloat16
NN = (((1,), (0,)), ((), ()))
NT = (((1,), (1,)), ((), ()))
XY_STEPS = sorted(
    [(dx, dy) for dx in range(4) for dy in range(4) if dx + dy > 0],
    key=lambda step: -sum(min(d, 4 - d) for d in step),
)
Z_STEPS = sorted(range(1, 16), key=lambda d: -min(d, 16 - d))


def dot(a, b, dims, precision=None):
    return lax.dot_general(a, b, dims, precision=precision, preferred_element_type=f32)


def halves(value):
    high = value.astype(bf16)
    low = (value - high.astype(f32)).astype(bf16)
    return jnp.concatenate([high, low], axis=0)


def fold(value):
    rows = value.shape[0] // 2
    return value[:rows] + value[rows:]


def inverse_factor(gram):
    n = gram.shape[0]
    rows = lax.broadcasted_iota(jnp.int32, (n, n), 0)
    cols = lax.broadcasted_iota(jnp.int32, (n, n), 1)
    left, right = gram, jnp.where(rows == cols, 1.0, 0.0).astype(f32)
    for j in range(n - 1):
        factor = left[:, j : j + 1] / left[j : j + 1, j : j + 1]
        factor = jnp.where(rows > j, factor, 0.0)
        left, right = left - factor * left[j : j + 1, :], right - factor * right[j : j + 1, :]
    pivots = jnp.sum(jnp.where(rows == cols, left, 0.0), axis=1, keepdims=True)
    return right / jnp.sqrt(pivots)


def wait_bytes(ref, sem):
    pltpu.make_async_copy(ref, ref, sem).wait()


def kernel(
    t0_in, t1_in, g_in, f_in, s_in, rb_out, m_out, linv_out,
    t0, t1, g, f, s, u, u_got, g_got, part, rsb, zbuf, pfull, mpart, rs2b, acc2, z2b, mine, linv, rb,
    load_sem, store_sem, u_sem, g_sem, rs_send, rs_recv, z_sem, ag_send, ag_recv, pair_sem, rs2_sem, z2_sem, ag2_sem,
):
    rem, div = lax.rem, lax.div
    dp, c, gen = lax.axis_index("dp"), lax.axis_index("mp"), lax.axis_index("gen")
    x, y, zlo = div(dp, 32), rem(dp, 4), rem(div(dp, 4), 8)
    z = gen * 8 + zlo
    me = x * 4 + y
    xs = [x] + [rem(x + d, 4) for d in range(1, 4)]
    ys = [y] + [rem(y + d, 4) for d in range(1, 4)]
    cs = [c, 1 - c]
    column = zlo * 4

    def plane(dx, dy, core):
        return (xs[dx] * 32 + column + ys[dy], core, gen)

    def along(dz):
        other = rem(z + dz, 16)
        return (x * 32 + rem(other, 8) * 4 + y, c, div(other, 8))

    partner = (dp, c, 1 - gen)

    def send(src, dst, send_sem, recv_sem, device):
        pltpu.make_async_remote_copy(
            src_ref=src, dst_ref=dst, send_sem=send_sem, recv_sem=recv_sem,
            device_id=device, device_id_type=MESH,
        ).start()

    loads = [
        pltpu.make_async_copy(s_in, s, load_sem.at[0]),
        pltpu.make_async_copy(g_in.at[0], g.at[0], load_sem.at[1]),
        pltpu.make_async_copy(g_in.at[1], g.at[1], load_sem.at[2]),
        pltpu.make_async_copy(t1_in, t1, load_sem.at[3]),
        pltpu.make_async_copy(f_in.at[1], f.at[1], load_sem.at[4]),
        pltpu.make_async_copy(f_in.at[0], f.at[0], load_sem.at[5]),
        pltpu.make_async_copy(t0_in, t0, load_sem.at[6]),
    ]
    for load in loads:
        load.start()

    barrier = pltpu.get_barrier_semaphore()
    peers = [along(dz) for dz in Z_STEPS] + [plane(*step, cs[k]) for step in XY_STEPS for k in range(2)]
    for peer in peers + [plane(0, 0, cs[1])]:
        pl.semaphore_signal(barrier, inc=1, device_id=peer, device_id_type=MESH)

    loads[0].wait()
    loads[1].wait()
    u_all = dot(s[0], g[0], NT)
    u[0] = u_all[:, :128]
    u[1] = u_all[:, 128:]
    u_copy = pltpu.make_async_remote_copy(
        src_ref=u.at[1 - gen], dst_ref=u_got, send_sem=u_sem.at[0], recv_sem=u_sem.at[1],
        device_id=partner, device_id_type=MESH,
    )

    g_copy = pltpu.make_async_remote_copy(
        src_ref=g.at[0, pl.ds(pl.multiple_of((1 - gen) * 128, 128), 128)], dst_ref=g_got,
        send_sem=g_sem.at[0], recv_sem=g_sem.at[1], device_id=partner, device_id_type=MESH,
    )

    @pl.when(gen == 1)
    def _():
        pl.semaphore_wait(barrier, 46)
        u_copy.start()

        @pl.when(c == 0)
        def _():
            g_copy.start()

    loads[2].wait()
    u1 = halves(dot(s[1], g[1], NT))
    loads[3].wait()
    loads[4].wait()
    for q in range(4):
        span = slice(384 * q, 384 * q + 384)
        block = fold(dot(u1, t1[:, span], NN)) + dot(s[1], f[1, span, :], NT)
        part[1, 4 * q : 4 * q + 4] = block.reshape(4, 8, 384)
    loads[5].wait()
    for q in range(4):
        span = slice(384 * q, 384 * q + 384)
        part[0, 4 * q : 4 * q + 4] = dot(s[0], f[0, span, :], NT).reshape(4, 8, 384)
    loads[6].wait()

    @pl.when(gen == 0)
    def _():
        pl.semaphore_wait(barrier, 46)
        u_copy.start()

        @pl.when(c == 0)
        def _():
            g_copy.start()

    def send_part(layer):
        other = rem(c + layer, 2)
        for dx, dy in XY_STEPS:
            send(
                part.at[layer, xs[dx] * 4 + ys[dy]], rsb.at[(dx * 4 + dy) * 2 + other],
                rs_send.at[layer], rs_recv, plane(dx, dy, layer),
            )

        @pl.when(other == 1)
        def _():
            send(part.at[layer, me], rsb.at[1], rs_send.at[layer], rs_recv, plane(0, 0, layer))

    def reduce_part(layer):
        wait_bytes(rsb.at[pl.ds(1, 31)], rs_recv)
        total = part[layer, me]
        for slot in range(1, 32):
            total = total + rsb[slot]
        zbuf[z] = total
        for dz in Z_STEPS:
            send(zbuf.at[z], zbuf.at[z], z_sem.at[0], z_sem.at[1], along(dz))

    def gather_power(layer):
        wait_bytes(zbuf.at[pl.ds(0, 15)], z_sem.at[1])
        total = zbuf[0]
        for slot in range(1, 16):
            total = total + zbuf[slot]
        pfull[layer, me] = total
        for step in XY_STEPS:
            send(pfull.at[layer, me], pfull.at[layer, me], ag_send, ag_recv, plane(*step, c))

    def wait_power(layer):
        forward = pltpu.make_async_remote_copy(
            src_ref=pfull.at[layer], dst_ref=pfull.at[layer],
            send_sem=pair_sem.at[0], recv_sem=pair_sem.at[1],
            device_id=plane(0, 0, cs[1]), device_id_type=MESH,
        )

        @pl.when(c == layer)
        def _():
            wait_bytes(pfull.at[layer, pl.ds(0, 15)], ag_recv)
            forward.start()

        @pl.when(c != layer)
        def _():
            forward.wait_recv()

    def power_block(layer, q):
        return pfull[layer, 4 * q : 4 * q + 4].reshape(32, 384)

    send_part(1)

    @pl.when((c == 1) & (gen == 1))
    def _():
        reduce_part(1)

    u_copy.wait()
    u0 = halves(u[gen] + u_got[...])
    for q in range(4):
        span = slice(384 * q, 384 * q + 384)
        block = fold(dot(u0, t0[:, span], NN)).reshape(4, 8, 384)
        part[0, 4 * q : 4 * q + 4] = part[0, 4 * q : 4 * q + 4] + block
    send_part(0)

    @pl.when(c == 1)
    def _():

        @pl.when(gen == 0)
        def _():
            reduce_part(1)

        g_copy.start()
        gather_power(1)

    @pl.when(c == 0)
    def _():
        reduce_part(0)
        gather_power(0)

    def products(layer, tokens):
        direct, by_token = None, None
        for q in range(4):
            span = slice(384 * q, 384 * q + 384)
            block = halves(power_block(layer, q))
            one = dot(block, f[layer, span, :], NN)
            two = dot(block, tokens[:, span], NT)
            direct = one if direct is None else direct + one
            by_token = two if by_token is None else by_token + two
        return fold(direct), halves(fold(by_token))

    def put(place, value):
        for q in range(3):
            mpart[4 * q : 4 * q + 4, place] = value[:, 128 * q : 128 * q + 128].reshape(4, 8, 128)

    def factorize(layer):
        gram = None
        for q in range(4):
            block = power_block(layer, q)
            one = dot(block, block, NT, HIGHEST)
            gram = one if gram is None else gram + one
        inverse = inverse_factor(gram)
        linv[layer] = inverse
        scaled = inverse * math.sqrt(1536)
        for q in range(4):
            rb[layer, :, 384 * q : 384 * q + 384] = dot(scaled, power_block(layer, q), NN, HIGHEST)

    rb_stores = [pltpu.make_async_copy(rb.at[i], rb_out.at[i], store_sem.at[i]) for i in range(2)]

    wait_power(1)
    direct, by_token = products(1, t1)
    put(1, direct + fold(dot(by_token, g[1], NN)))

    g_copy.wait()
    wait_power(0)
    direct, by_token = products(0, t0)
    own_rows = g[0, pl.ds(pl.multiple_of(gen * 128, 128), 128), :]
    put(0, direct + fold(dot(by_token, own_rows, NN)))
    put(2, fold(dot(by_token, g_got[...], NN)))

    for dx, dy in XY_STEPS:

        @pl.when(xs[dx] < 3)
        def _():
            send(
                mpart.at[xs[dx] * 4 + ys[dy]], rs2b.at[dx * 4 + dy],
                rs2_sem.at[0], rs2_sem.at[1], plane(dx, dy, c),
            )

    factorize(0)
    rb_stores[0].start()

    @pl.when(x < 3)
    def _():
        wait_bytes(rs2b.at[pl.ds(1, 15)], rs2_sem.at[1])
        total = mpart[me]
        for slot in range(1, 16):
            total = total + rs2b[slot]
        acc2[...] = total
        z2b[z] = total[:2]

        for dz in Z_STEPS:
            where = along(dz)

            @pl.when(where[2] == gen)
            def _():
                send(acc2.at[pl.ds(0, 2)], z2b.at[z], z2_sem.at[0], z2_sem.at[1], where)

            @pl.when(where[2] != gen)
            def _():
                send(acc2.at[2], z2b.at[z, 0], z2_sem.at[2], z2_sem.at[3], where)

    factorize(1)
    rb_stores[1].start()
    linv_store = pltpu.make_async_copy(linv, linv_out, store_sem.at[3])
    linv_store.start()

    @pl.when(x < 3)
    def _():
        wait_bytes(z2b.at[pl.ds(0, 7)], z2_sem.at[1])
        wait_bytes(z2b.at[pl.ds(0, 4)], z2_sem.at[3])
        first = z2b[0, 0]
        for slot in range(1, 16):
            first = first + z2b[slot, 0]
        second = z2b[gen * 8, 1]
        for slot in range(1, 8):
            second = second + z2b[gen * 8 + slot, 1]
        mine[0] = first
        mine[1] = second

        for step in XY_STEPS:
            send(mine, m_out.at[me], ag2_sem.at[0], ag2_sem.at[1], plane(*step, c))
        keep = pltpu.make_async_copy(mine, m_out.at[me], store_sem.at[2])
        keep.start()
        wait_bytes(m_out.at[pl.ds(0, 11)], ag2_sem.at[1])
        keep.wait()

    @pl.when(x == 3)
    def _():
        wait_bytes(m_out.at[pl.ds(0, 12)], ag2_sem.at[1])

    for layer in range(2):

        @pl.when(c == layer)
        def _():
            wait_bytes(part.at[layer, pl.ds(0, 15)], rs_send.at[layer])

        @pl.when(c != layer)
        def _():
            wait_bytes(part.at[layer, pl.ds(0, 16)], rs_send.at[layer])

    wait_bytes(zbuf.at[pl.ds(0, 15)], z_sem.at[0])
    wait_bytes(rsb.at[pl.ds(0, 15)], ag_send)
    wait_bytes(rsb.at[pl.ds(0, 16)], pair_sem.at[0])

    @pl.when(x < 3)
    def _():
        wait_bytes(mpart.at[pl.ds(0, 11)], rs2_sem.at[0])
        wait_bytes(z2b.at[pl.ds(0, 7)], z2_sem.at[0])
        wait_bytes(z2b.at[pl.ds(0, 4)], z2_sem.at[2])
        wait_bytes(rs2b.at[pl.ds(0, 10)], ag2_sem.at[0])

    @pl.when(x == 3)
    def _():
        wait_bytes(mpart.at[pl.ds(0, 12)], rs2_sem.at[0])

    rb_stores[0].wait()
    rb_stores[1].wait()
    linv_store.wait()


def write_out(rb_in, sums_in, inverse_in, rb_out, cf_out, rb, sums, inverse, cf, sem):
    sums_load = pltpu.make_async_copy(sums_in, sums, sem.at[0])
    inverse_load = pltpu.make_async_copy(inverse_in, inverse, sem.at[1])
    rb_load = pltpu.make_async_copy(rb_in, rb, sem.at[2])
    rb_copy = pltpu.make_async_copy(rb, rb_out, sem.at[3])
    cf_copy = pltpu.make_async_copy(cf, cf_out, sem.at[4])
    sums_load.start()
    inverse_load.start()
    rb_load.start()
    sums_load.wait()
    inverse_load.wait()
    for layer in range(2):
        scaled = inverse[layer] * (1.0 / 128.0)
        for q in range(3):
            block = sums[4 * q : 4 * q + 4, layer].reshape(32, 128)
            cf[layer, :, 128 * q : 128 * q + 128] = dot(scaled, block, NN, HIGHEST)
    cf_copy.start()
    rb_load.wait()
    rb_copy.start()
    cf_copy.wait()
    rb_copy.wait()


def local(fresh_tokens, saved_tokens, cotangents, feedback, start_factors):
    anywhere = pl.BlockSpec(memory_space=pl.ANY)
    vmem, dma = pltpu.VMEM, pltpu.SemaphoreType.DMA
    rb, sums, inverse = pl.pallas_call(
        kernel,
        out_shape=(
            jax.ShapeDtypeStruct((2, 32, 1536), f32),
            jax.ShapeDtypeStruct((12, 2, 8, 128), f32),
            jax.ShapeDtypeStruct((2, 32, 32), f32),
        ),
        in_specs=[anywhere] * 5,
        out_specs=(anywhere, anywhere, anywhere),
        scratch_shapes=[
            vmem((128, 1536), bf16),
            vmem((256, 1536), bf16),
            vmem((2, 256, 384), bf16),
            vmem((2, 1536, 384), bf16),
            vmem((2, 32, 384), bf16),
            vmem((2, 32, 128), f32),
            vmem((32, 128), f32),
            vmem((128, 384), bf16),
            vmem((2, 16, 8, 384), f32),
            vmem((32, 8, 384), f32),
            vmem((16, 8, 384), f32),
            vmem((2, 16, 8, 384), f32),
            vmem((12, 3, 8, 128), f32),
            vmem((16, 3, 8, 128), f32),
            vmem((3, 8, 128), f32),
            vmem((16, 2, 8, 128), f32),
            vmem((2, 8, 128), f32),
            vmem((2, 32, 32), f32),
            vmem((2, 32, 1536), f32),
            dma((7,)),
            dma((4,)),
            dma((2,)),
            dma((2,)),
            dma((2,)),
            dma,
            dma((2,)),
            dma,
            dma,
            dma((2,)),
            dma((2,)),
            dma((4,)),
            dma((2,)),
        ],
        compiler_params=pltpu.CompilerParams(
            collective_id=0, has_side_effects=True, vmem_limit_bytes=60 * 2**20
        ),
        cost_estimate=pl.CostEstimate(flops=10**9, bytes_accessed=5 * 10**6, transcendentals=0),
        name="compress",
    )(
        fresh_tokens,
        saved_tokens,
        cotangents,
        feedback.reshape(2, 1536, 384),
        jnp.transpose(start_factors, (0, 2, 1)),
    )
    rb, cf = pl.pallas_call(
        write_out,
        out_shape=(
            jax.ShapeDtypeStruct((2, 32, 1536), f32),
            jax.ShapeDtypeStruct((2, 32, 384), f32),
        ),
        in_specs=[anywhere] * 3,
        out_specs=(anywhere, anywhere),
        scratch_shapes=[
            vmem((2, 32, 1536), f32),
            vmem((12, 2, 8, 128), f32),
            vmem((2, 32, 32), f32),
            vmem((2, 32, 384), f32),
            dma((5,)),
        ],
        name="write_out",
    )(rb, sums, inverse)
    return jnp.transpose(rb, (0, 2, 1)), jnp.transpose(cf, (0, 2, 1))


def solution(mesh):
    return jax.shard_map(
        local,
        mesh=mesh,
        in_specs=(
            P(("dp", "gen"), None),
            P("dp", None),
            P(None, "dp", ("mp", "gen")),
            P(None, "dp", None, ("mp", "gen")),
            P(None, ("mp", "gen"), None),
        ),
        out_specs=(P(), P(None, ("mp", "gen"), None)),
        check_vma=False,
    )
```

```python
import math

import jax
import jax.numpy as jnp
from jax import lax
from jax.experimental import pallas as pl
from jax.experimental.pallas import tpu as pltpu
from jax.sharding import PartitionSpec as P

MESH = pl.DeviceIdType.MESH
HIGHEST = lax.Precision.HIGHEST
f32, bf16 = jnp.float32, jnp.bfloat16
NN = (((1,), (0,)), ((), ()))
NT = (((1,), (1,)), ((), ()))
XY_STEPS = sorted(
    [(dx, dy) for dx in range(4) for dy in range(4) if dx + dy > 0],
    key=lambda step: -sum(min(d, 4 - d) for d in step),
)
Z_STEPS = sorted(range(1, 16), key=lambda d: -min(d, 16 - d))


def dot(a, b, dims, precision=None):
    return lax.dot_general(a, b, dims, precision=precision, preferred_element_type=f32)


def halves(value):
    high = value.astype(bf16)
    low = (value - high.astype(f32)).astype(bf16)
    return jnp.concatenate([high, low], axis=0)


def fold(value):
    rows = value.shape[0] // 2
    return value[:rows] + value[rows:]


def inverse_factor(gram):
    n = gram.shape[0]
    rows = lax.broadcasted_iota(jnp.int32, (n, n), 0)
    cols = lax.broadcasted_iota(jnp.int32, (n, n), 1)
    left, right = gram, jnp.where(rows == cols, 1.0, 0.0).astype(f32)
    for j in range(n - 1):
        factor = left[:, j : j + 1] / left[j : j + 1, j : j + 1]
        factor = jnp.where(rows > j, factor, 0.0)
        left, right = left - factor * left[j : j + 1, :], right - factor * right[j : j + 1, :]
    pivots = jnp.sum(jnp.where(rows == cols, left, 0.0), axis=1, keepdims=True)
    return right / jnp.sqrt(pivots)


def wait_bytes(ref, sem):
    pltpu.make_async_copy(ref, ref, sem).wait()


def kernel(
    t0_in, t1_in, g_in, f_in, s_in, rb_out, m_out, linv_out,
    t0, t1, g, f, s, u, u_got, g_got, part, rsb, zbuf, pfull, mpart, rs2b, acc2, z2b, mine, linv, rb,
    load_sem, store_sem, u_sem, g_sem, rs_send, rs_recv, z_sem, ag_send, ag_recv, pair_sem, rs2_sem, z2_sem, ag2_sem,
):
    rem, div = lax.rem, lax.div
    dp, c, gen = lax.axis_index("dp"), lax.axis_index("mp"), lax.axis_index("gen")
    x, y, zlo = div(dp, 32), rem(dp, 4), rem(div(dp, 4), 8)
    z = gen * 8 + zlo
    me = x * 4 + y
    xs = [x] + [rem(x + d, 4) for d in range(1, 4)]
    ys = [y] + [rem(y + d, 4) for d in range(1, 4)]
    cs = [c, 1 - c]
    column = zlo * 4

    def plane(dx, dy, core):
        return (xs[dx] * 32 + column + ys[dy], core, gen)

    def along(dz):
        other = rem(z + dz, 16)
        return (x * 32 + rem(other, 8) * 4 + y, c, div(other, 8))

    partner = (dp, c, 1 - gen)

    def send(src, dst, send_sem, recv_sem, device):
        pltpu.make_async_remote_copy(
            src_ref=src, dst_ref=dst, send_sem=send_sem, recv_sem=recv_sem,
            device_id=device, device_id_type=MESH,
        ).start()

    loads = [
        pltpu.make_async_copy(s_in, s, load_sem.at[0]),
        pltpu.make_async_copy(g_in.at[0], g.at[0], load_sem.at[1]),
        pltpu.make_async_copy(g_in.at[1], g.at[1], load_sem.at[2]),
        pltpu.make_async_copy(t1_in, t1, load_sem.at[3]),
        pltpu.make_async_copy(f_in.at[1], f.at[1], load_sem.at[4]),
        pltpu.make_async_copy(f_in.at[0], f.at[0], load_sem.at[5]),
        pltpu.make_async_copy(t0_in, t0, load_sem.at[6]),
    ]
    barrier = pltpu.get_barrier_semaphore()
    peers = [along(dz) for dz in Z_STEPS] + [plane(*step, cs[k]) for step in XY_STEPS for k in range(2)]
    for peer in peers + [plane(0, 0, cs[1])]:
        pl.semaphore_signal(barrier, inc=1, device_id=peer, device_id_type=MESH)

    for load in loads:
        load.start()

    loads[0].wait()
    loads[1].wait()
    u_all = dot(s[0], g[0], NT)
    u[0] = u_all[:, :128]
    u[1] = u_all[:, 128:]
    u_copy = pltpu.make_async_remote_copy(
        src_ref=u.at[1 - gen], dst_ref=u_got, send_sem=u_sem.at[0], recv_sem=u_sem.at[1],
        device_id=partner, device_id_type=MESH,
    )

    g_copy = pltpu.make_async_remote_copy(
        src_ref=g.at[0, pl.ds(pl.multiple_of((1 - gen) * 128, 128), 128)], dst_ref=g_got,
        send_sem=g_sem.at[0], recv_sem=g_sem.at[1], device_id=partner, device_id_type=MESH,
    )

    @pl.when(gen == 1)
    def _():
        pl.semaphore_wait(barrier, 46)
        u_copy.start()

        @pl.when(c == 0)
        def _():
            g_copy.start()

    loads[2].wait()
    u1 = halves(dot(s[1], g[1], NT))
    loads[3].wait()
    loads[4].wait()
    for q in range(4):
        span = slice(384 * q, 384 * q + 384)
        block = fold(dot(u1, t1[:, span], NN)) + dot(s[1], f[1, span, :], NT)
        part[1, 4 * q : 4 * q + 4] = block.reshape(4, 8, 384)
    loads[5].wait()
    for q in range(4):
        span = slice(384 * q, 384 * q + 384)
        part[0, 4 * q : 4 * q + 4] = dot(s[0], f[0, span, :], NT).reshape(4, 8, 384)
    loads[6].wait()

    @pl.when(gen == 0)
    def _():
        pl.semaphore_wait(barrier, 46)
        u_copy.start()

        @pl.when(c == 0)
        def _():
            g_copy.start()

    def send_part(layer):
        other = rem(c + layer, 2)
        for dx, dy in XY_STEPS:
            send(
                part.at[layer, xs[dx] * 4 + ys[dy]], rsb.at[(dx * 4 + dy) * 2 + other],
                rs_send.at[layer], rs_recv, plane(dx, dy, layer),
            )

        @pl.when(other == 1)
        def _():
            send(part.at[layer, me], rsb.at[1], rs_send.at[layer], rs_recv, plane(0, 0, layer))

    def reduce_part(layer):
        wait_bytes(rsb.at[pl.ds(1, 31)], rs_recv)
        total = part[layer, me]
        for slot in range(1, 32):
            total = total + rsb[slot]
        zbuf[z] = total
        for dz in Z_STEPS:
            send(zbuf.at[z], zbuf.at[z], z_sem.at[0], z_sem.at[1], along(dz))

    def gather_power(layer):
        wait_bytes(zbuf.at[pl.ds(0, 15)], z_sem.at[1])
        total = zbuf[0]
        for slot in range(1, 16):
            total = total + zbuf[slot]
        pfull[layer, me] = total
        for step in XY_STEPS:
            send(pfull.at[layer, me], pfull.at[layer, me], ag_send, ag_recv, plane(*step, c))

    def wait_power(layer):
        forward = pltpu.make_async_remote_copy(
            src_ref=pfull.at[layer], dst_ref=pfull.at[layer],
            send_sem=pair_sem.at[0], recv_sem=pair_sem.at[1],
            device_id=plane(0, 0, cs[1]), device_id_type=MESH,
        )

        @pl.when(c == layer)
        def _():
            wait_bytes(pfull.at[layer, pl.ds(0, 15)], ag_recv)
            forward.start()

        @pl.when(c != layer)
        def _():
            forward.wait_recv()

    def power_block(layer, q):
        return pfull[layer, 4 * q : 4 * q + 4].reshape(32, 384)

    send_part(1)

    @pl.when((c == 1) & (gen == 1))
    def _():
        reduce_part(1)

    u_copy.wait()
    u0 = halves(u[gen] + u_got[...])
    for q in range(4):
        span = slice(384 * q, 384 * q + 384)
        block = fold(dot(u0, t0[:, span], NN)).reshape(4, 8, 384)
        part[0, 4 * q : 4 * q + 4] = part[0, 4 * q : 4 * q + 4] + block
    send_part(0)

    @pl.when(c == 1)
    def _():

        @pl.when(gen == 0)
        def _():
            reduce_part(1)

        g_copy.start()
        gather_power(1)

    @pl.when(c == 0)
    def _():
        reduce_part(0)
        gather_power(0)

    def products(layer, tokens):
        direct, by_token = None, None
        for q in range(4):
            span = slice(384 * q, 384 * q + 384)
            block = halves(power_block(layer, q))
            one = dot(block, f[layer, span, :], NN)
            two = dot(block, tokens[:, span], NT)
            direct = one if direct is None else direct + one
            by_token = two if by_token is None else by_token + two
        return fold(direct), halves(fold(by_token))

    def put(place, value):
        for q in range(3):
            mpart[4 * q : 4 * q + 4, place] = value[:, 128 * q : 128 * q + 128].reshape(4, 8, 128)

    def factorize(layer):
        gram = None
        for q in range(4):
            block = power_block(layer, q)
            one = dot(block, block, NT, HIGHEST)
            gram = one if gram is None else gram + one
        inverse = inverse_factor(gram)
        linv[layer] = inverse
        scaled = inverse * math.sqrt(1536)
        for q in range(4):
            rb[layer, :, 384 * q : 384 * q + 384] = dot(scaled, power_block(layer, q), NN, HIGHEST)

    rb_stores = [pltpu.make_async_copy(rb.at[i], rb_out.at[i], store_sem.at[i]) for i in range(2)]

    wait_power(1)
    direct, by_token = products(1, t1)
    put(1, direct + fold(dot(by_token, g[1], NN)))

    g_copy.wait()
    wait_power(0)
    direct, by_token = products(0, t0)
    own_rows = g[0, pl.ds(pl.multiple_of(gen * 128, 128), 128), :]
    put(0, direct + fold(dot(by_token, own_rows, NN)))
    put(2, fold(dot(by_token, g_got[...], NN)))

    for dx, dy in XY_STEPS:

        @pl.when(xs[dx] < 3)
        def _():
            send(
                mpart.at[xs[dx] * 4 + ys[dy]], rs2b.at[dx * 4 + dy],
                rs2_sem.at[0], rs2_sem.at[1], plane(dx, dy, c),
            )

    factorize(0)
    rb_stores[0].start()

    @pl.when(x < 3)
    def _():
        wait_bytes(rs2b.at[pl.ds(1, 15)], rs2_sem.at[1])
        total = mpart[me]
        for slot in range(1, 16):
            total = total + rs2b[slot]
        acc2[...] = total
        z2b[z] = total[:2]

        for dz in Z_STEPS:
            where = along(dz)

            @pl.when(where[2] == gen)
            def _():
                send(acc2.at[pl.ds(0, 2)], z2b.at[z], z2_sem.at[0], z2_sem.at[1], where)

            @pl.when(where[2] != gen)
            def _():
                send(acc2.at[2], z2b.at[z, 0], z2_sem.at[2], z2_sem.at[3], where)

    factorize(1)
    rb_stores[1].start()
    linv_store = pltpu.make_async_copy(linv, linv_out, store_sem.at[3])
    linv_store.start()

    @pl.when(x < 3)
    def _():
        wait_bytes(z2b.at[pl.ds(0, 7)], z2_sem.at[1])
        wait_bytes(z2b.at[pl.ds(0, 4)], z2_sem.at[3])
        first = z2b[0, 0]
        for slot in range(1, 16):
            first = first + z2b[slot, 0]
        second = z2b[gen * 8, 1]
        for slot in range(1, 8):
            second = second + z2b[gen * 8 + slot, 1]
        mine[0] = first
        mine[1] = second

        for step in XY_STEPS:
            send(mine, m_out.at[me], ag2_sem.at[0], ag2_sem.at[1], plane(*step, c))
        keep = pltpu.make_async_copy(mine, m_out.at[me], store_sem.at[2])
        keep.start()
        wait_bytes(m_out.at[pl.ds(0, 11)], ag2_sem.at[1])
        keep.wait()

    @pl.when(x == 3)
    def _():
        wait_bytes(m_out.at[pl.ds(0, 12)], ag2_sem.at[1])

    for layer in range(2):

        @pl.when(c == layer)
        def _():
            wait_bytes(part.at[layer, pl.ds(0, 15)], rs_send.at[layer])

        @pl.when(c != layer)
        def _():
            wait_bytes(part.at[layer, pl.ds(0, 16)], rs_send.at[layer])

    wait_bytes(zbuf.at[pl.ds(0, 15)], z_sem.at[0])
    wait_bytes(rsb.at[pl.ds(0, 15)], ag_send)
    wait_bytes(rsb.at[pl.ds(0, 16)], pair_sem.at[0])

    @pl.when(x < 3)
    def _():
        wait_bytes(mpart.at[pl.ds(0, 11)], rs2_sem.at[0])
        wait_bytes(z2b.at[pl.ds(0, 7)], z2_sem.at[0])
        wait_bytes(z2b.at[pl.ds(0, 4)], z2_sem.at[2])
        wait_bytes(rs2b.at[pl.ds(0, 10)], ag2_sem.at[0])

    @pl.when(x == 3)
    def _():
        wait_bytes(mpart.at[pl.ds(0, 12)], rs2_sem.at[0])

    rb_stores[0].wait()
    rb_stores[1].wait()
    linv_store.wait()


def write_out(rb_in, sums_in, inverse_in, rb_out, cf_out, rb, sums, inverse, cf, sem):
    sums_load = pltpu.make_async_copy(sums_in, sums, sem.at[0])
    inverse_load = pltpu.make_async_copy(inverse_in, inverse, sem.at[1])
    rb_load = pltpu.make_async_copy(rb_in, rb, sem.at[2])
    rb_copy = pltpu.make_async_copy(rb, rb_out, sem.at[3])
    cf_copy = pltpu.make_async_copy(cf, cf_out, sem.at[4])
    sums_load.start()
    inverse_load.start()
    rb_load.start()
    sums_load.wait()
    inverse_load.wait()
    for layer in range(2):
        scaled = inverse[layer] * (1.0 / 128.0)
        for q in range(3):
            block = sums[4 * q : 4 * q + 4, layer].reshape(32, 128)
            cf[layer, :, 128 * q : 128 * q + 128] = dot(scaled, block, NN, HIGHEST)
    cf_copy.start()
    rb_load.wait()
    rb_copy.start()
    cf_copy.wait()
    rb_copy.wait()


def local(fresh_tokens, saved_tokens, cotangents, feedback, start_factors):
    anywhere = pl.BlockSpec(memory_space=pl.ANY)
    vmem, dma = pltpu.VMEM, pltpu.SemaphoreType.DMA
    rb, sums, inverse = pl.pallas_call(
        kernel,
        out_shape=(
            jax.ShapeDtypeStruct((2, 32, 1536), f32),
            jax.ShapeDtypeStruct((12, 2, 8, 128), f32),
            jax.ShapeDtypeStruct((2, 32, 32), f32),
        ),
        in_specs=[anywhere] * 5,
        out_specs=(anywhere, anywhere, anywhere),
        scratch_shapes=[
            vmem((128, 1536), bf16),
            vmem((256, 1536), bf16),
            vmem((2, 256, 384), bf16),
            vmem((2, 1536, 384), bf16),
            vmem((2, 32, 384), bf16),
            vmem((2, 32, 128), f32),
            vmem((32, 128), f32),
            vmem((128, 384), bf16),
            vmem((2, 16, 8, 384), f32),
            vmem((32, 8, 384), f32),
            vmem((16, 8, 384), f32),
            vmem((2, 16, 8, 384), f32),
            vmem((12, 3, 8, 128), f32),
            vmem((16, 3, 8, 128), f32),
            vmem((3, 8, 128), f32),
            vmem((16, 2, 8, 128), f32),
            vmem((2, 8, 128), f32),
            vmem((2, 32, 32), f32),
            vmem((2, 32, 1536), f32),
            dma((7,)),
            dma((4,)),
            dma((2,)),
            dma((2,)),
            dma((2,)),
            dma,
            dma((2,)),
            dma,
            dma,
            dma((2,)),
            dma((2,)),
            dma((4,)),
            dma((2,)),
        ],
        compiler_params=pltpu.CompilerParams(
            collective_id=0, has_side_effects=True, vmem_limit_bytes=60 * 2**20
        ),
        cost_estimate=pl.CostEstimate(flops=10**9, bytes_accessed=5 * 10**6, transcendentals=0),
        name="compress",
    )(
        fresh_tokens,
        saved_tokens,
        cotangents,
        feedback.reshape(2, 1536, 384),
        jnp.transpose(start_factors, (0, 2, 1)),
    )
    rb, cf = pl.pallas_call(
        write_out,
        out_shape=(
            jax.ShapeDtypeStruct((2, 32, 1536), f32),
            jax.ShapeDtypeStruct((2, 32, 384), f32),
        ),
        in_specs=[anywhere] * 3,
        out_specs=(anywhere, anywhere),
        scratch_shapes=[
            vmem((2, 32, 1536), f32),
            vmem((12, 2, 8, 128), f32),
            vmem((2, 32, 32), f32),
            vmem((2, 32, 384), f32),
            dma((5,)),
        ],
        name="write_out",
    )(rb, sums, inverse)
    return jnp.transpose(rb, (0, 2, 1)), jnp.transpose(cf, (0, 2, 1))


def solution(mesh):
    return jax.shard_map(
        local,
        mesh=mesh,
        in_specs=(
            P(("dp", "gen"), None),
            P("dp", None),
            P(None, "dp", ("mp", "gen")),
            P(None, "dp", None, ("mp", "gen")),
            P(None, ("mp", "gen"), None),
        ),
        out_specs=(P(), P(None, ("mp", "gen"), None)),
        check_vma=False,
    )
```
